32 devices in a mesh: groups: 2 (over y), dp: 4 (over z), tensor: 4 (over x, core).
Axes of the slice: x: 2, y: 2, z: 4, core: 2. Of those that a mesh axis runs over, the one named last changes fastest.
Arguments:
- normed: bfloat16 [2048, 8192], P(('groups', 'dp'), 'tensor'), parts along dimension 0, may hold values from -6 to 6
- grad_key: bfloat16 [2048, 1024], P(('groups', 'dp'), 'tensor'), parts along dimension 0, may hold values from -6 to 6
- grad_value: bfloat16 [2048, 1024], P(('groups', 'dp'), 'tensor'), parts along dimension 0, may hold values from -6 to 6
- weight_key: bfloat16 [8192, 1024], P('dp', 'tensor'), may hold values from -0.1875 to 0.1875
- weight_value: bfloat16 [8192, 1024], P('dp', 'tensor'), may hold values from -0.1875 to 0.1875
- proj_in: bfloat16 [8192, 128], P('tensor'), may hold values from -0.0625 to 0.0625
- proj_out: bfloat16 [2, 1024, 64], P(None, 'tensor'), may hold values from -0.1875 to 0.1875
- lengths: int32 [8], P(('groups', 'dp')), parts along dimension 0, may hold values from 64 to 256
- queries: bfloat16 [512, 2, 4096], P('dp', None, 'tensor'), may hold values from -6 to 6
Outputs:
- grad_input: bfloat16 [2048, 8192], P(('groups', 'dp'), 'tensor'), parts along dimension 0
- scores: float32 [512, 8], P('dp', 'groups'), parts along dimension 1
The draws below stay inside these ranges and needn't reach their ends.
There are 2 independent parts, one for each index of `groups`. The reference program is written for one: setup_inputs(seed, part) draws one part's arguments, and reference() takes and returns one part's arrays. A program takes and returns all parts, laid end to end along the dimension named above; an argument that names none is the same for every part. Nothing has to cross between parts.
All inputs are finite; a program needn't handle non-finite values.
Results may differ from the reference program's by a relative error of at most 0.018.
Values may be sent and summed in bfloat16 or wider, within the bound.
A program may use at most 64 MiB of HBM per device.

```python
import jax
import jax.numpy as jnp
from jax import lax

D = 8192
KVD = 1024
R = 64
LEN = 256
TOKENS = 1024
SEQS = 4
NQ = 512
N_TENSOR = 4


def set_ends(result, own_key, low, top_value):
    longest = result.shape.index(max(result.shape))
    spots = []
    for shift in (0, 1):
        where = [jax.random.randint(jax.random.fold_in(own_key, axis), (), 0, length) for axis, length in enumerate(result.shape)]
        where[longest] = (where[longest] + shift) % result.shape[longest]
        spots.append(tuple(where))
    return result.at[spots[0]].set(low).at[spots[1]].set(top_value)


def block_levels(stream_key, dims, cuts, least, high):
    level = 1.0
    for position, parts in cuts:
        draws = jax.random.uniform(jax.random.fold_in(jax.random.fold_in(stream_key, 6), position), (parts,), jnp.float32, least / len(cuts), high / len(cuts))
        level = level * jnp.repeat(jnp.exp(draws), dims[position] // parts).reshape((-1,) + (1,) * (len(dims) - 1 - position))
    return level


def gaussian(stream_key, extent, spread, limit, shards=(), kind=jnp.bfloat16):
    array = spread * jax.random.normal(stream_key, extent, jnp.float32)
    if shards:
        array = array * block_levels(stream_key, extent, shards, -0.22, 0.18)
    return jnp.clip(array, -limit, limit).astype(kind)


def setup_inputs(seed: int = 0, part: int = 0) -> dict:
    seeds = jax.random.split(jax.random.key(seed), 10)
    part_splits = jax.random.split(jax.random.fold_in(seeds[9], part), 10)
    return {
        "normed": gaussian(part_splits[0], (TOKENS, D), 1.0, 6.0, ((0, 4), (1, 4))),
        "grad_key": gaussian(part_splits[1], (TOKENS, KVD), 1.0, 6.0, ((0, 4), (1, 4))),
        "grad_value": gaussian(part_splits[2], (TOKENS, KVD), 1.0, 6.0, ((0, 4), (1, 4))),
        "weight_key": gaussian(seeds[3], (D, KVD), KVD ** -0.5, 0.1875, ((0, 4), (1, 4))),
        "weight_value": gaussian(seeds[4], (D, KVD), KVD ** -0.5, 0.1875, ((0, 4), (1, 4))),
        "proj_in": gaussian(seeds[5], (D, 2 * R), D ** -0.5, 0.0625, ((0, 4),)),
        "proj_out": gaussian(seeds[6], (2, KVD, R), KVD ** -0.5, 0.1875, ((1, 4),)),
        "lengths": set_ends(jax.random.randint(part_splits[7], (SEQS,), LEN // 4, LEN + 1), jax.random.fold_in(part_splits[7], 1), LEN // 4, LEN).astype(jnp.int32),
        "queries": gaussian(seeds[8], (NQ, 2, R * R), 1.0, 6.0, ((0, 4), (2, 4))),
    }


def reference(normed, grad_key, grad_value, weight_key, weight_value, proj_in, proj_out, lengths, queries):
    cols = KVD // N_TENSOR
    grads = jnp.concatenate([grad_key.reshape(TOKENS, N_TENSOR, cols), grad_value.reshape(TOKENS, N_TENSOR, cols)], axis=2)
    weights = jnp.concatenate([weight_key.reshape(D, N_TENSOR, cols), weight_value.reshape(D, N_TENSOR, cols)], axis=2)

    def add_group(total, group):
        grad_part = lax.dynamic_index_in_dim(grads, group, 1, keepdims=False)
        weight_part = lax.dynamic_index_in_dim(weights, group, 1, keepdims=False)
        part = lax.dot_general(grad_part, weight_part, (((1,), (1,)), ((), ())), preferred_element_type=jnp.float32)
        part = lax.optimization_barrier(part.astype(jnp.bfloat16))
        return (total + part.astype(jnp.float32), None)
    total, _ = lax.scan(add_group, jnp.zeros((TOKENS, D), jnp.float32), jnp.arange(N_TENSOR, dtype=jnp.int32))
    grad_input = total.astype(jnp.bfloat16)
    in_sketch = jnp.dot(normed, proj_in, preferred_element_type=jnp.float32).astype(jnp.bfloat16)
    out_key = jnp.dot(grad_key, proj_out[0], preferred_element_type=jnp.float32)
    out_value = jnp.dot(grad_value, proj_out[1], preferred_element_type=jnp.float32)
    out_sketch = jnp.stack([out_key, out_value], axis=1).astype(jnp.bfloat16)
    positions = jnp.arange(LEN, dtype=jnp.int32)
    live = (positions[None, :] < lengths[:, None]).astype(jnp.float32)
    in_seq = in_sketch.astype(jnp.float32).reshape(SEQS, LEN, 2, R)
    out_seq = out_sketch.astype(jnp.float32).reshape(SEQS, LEN, 2, R) * live[:, :, None, None]
    sums = jnp.einsum('stla,stlb->slab', out_seq, in_seq)
    scale = 1.0 / jnp.sqrt(lengths.astype(jnp.float32))
    seq_sketch = (sums * scale[:, None, None, None]).astype(jnp.bfloat16).reshape(SEQS, 2, R * R)
    scores = jnp.einsum('qlf,slf->qs', queries.astype(jnp.float32), seq_sketch.astype(jnp.float32)) / R
    return (grad_input, scores)
```

```python
import jax
import jax.numpy as jnp
from jax import lax
from jax.sharding import PartitionSpec as P


def by_tokens(grads, weights):
    partial_grad = lax.dot_general(
        grads,
        lax.all_gather(weights, "dp", axis=0, tiled=True),
        (((1,), (1,)), ((), ())),
        preferred_element_type=jnp.float32,
    )
    return lax.psum_scatter(
        partial_grad.astype(jnp.bfloat16), "tensor", scatter_dimension=1, tiled=True
    )


def by_features(grads, weights):
    n = lax.axis_size("dp")
    partial_grad = lax.dot_general(
        lax.all_gather(grads, "dp", axis=0, tiled=True),
        weights,
        (((1,), (1,)), ((), ())),
        preferred_element_type=jnp.float32,
    )
    mine = lax.psum_scatter(
        partial_grad.astype(jnp.bfloat16), "tensor", scatter_dimension=0, tiled=True
    )
    turn = [(d * n + t, t * n + d) for d in range(n) for t in range(n)]
    return lax.ppermute(mine, ("dp", "tensor"), turn)


def body(
    normed, grad_key, grad_value, weight_key, weight_value, proj_in, proj_out, lengths, queries
):
    grads = jnp.concatenate([grad_key, grad_value], axis=1)
    weights = jnp.concatenate([weight_key, weight_value], axis=1)
    if lax.axis_size("dp") == lax.axis_size("tensor"):
        grad_input = by_features(grads, weights)
    else:
        grad_input = by_tokens(grads, weights)
    tokens = normed.shape[0]
    rank = proj_out.shape[2]
    shards = lax.axis_size("tensor")
    own_rows = rank // shards
    in_part = jnp.dot(normed, proj_in, preferred_element_type=jnp.float32)
    out_part = jnp.stack(
        [
            jnp.dot(grad_key, proj_out[0], preferred_element_type=jnp.float32),
            jnp.dot(grad_value, proj_out[1], preferred_element_type=jnp.float32),
        ],
        axis=1,
    )
    in_whole, out_whole = (
        lax.psum(in_part.astype(jnp.bfloat16), "tensor").astype(jnp.float32),
        lax.psum(out_part.astype(jnp.bfloat16), "tensor").astype(jnp.float32),
    )
    out_own = lax.dynamic_slice_in_dim(out_whole, lax.axis_index("tensor") * own_rows, own_rows, 2)
    in_sketch = in_whole.astype(jnp.bfloat16)
    out_sketch = out_own.astype(jnp.bfloat16)
    seq_count = lengths.shape[0]
    seq_len = tokens // seq_count
    positions = lax.broadcasted_iota(jnp.int32, (seq_count, seq_len), 1)
    live = (positions < lengths[:, None]).astype(jnp.bfloat16)
    in_seq = in_sketch.reshape(seq_count, seq_len, 2, rank)
    out_seq = out_sketch.reshape(seq_count, seq_len, 2, own_rows) * live[:, :, None, None]
    sums = jnp.einsum("stla,stlb->slab", out_seq, in_seq, preferred_element_type=jnp.float32)
    scale = 1.0 / jnp.sqrt(lengths.astype(jnp.float32))
    seq_sketch = (
        (sums * scale[:, None, None, None])
        .astype(jnp.bfloat16)
        .reshape(seq_count, 2, own_rows * rank)
    )
    partial_scores = jnp.einsum(
        "qlf,slf->qs",
        queries,
        lax.all_gather(seq_sketch, "dp", axis=0, tiled=True),
        preferred_element_type=jnp.float32,
    )
    scores = lax.psum(partial_scores, "tensor") / rank
    return (grad_input, scores)


def solution(mesh):
    in_specs = (
        P(("groups", "dp"), "tensor"),
        P(("groups", "dp"), "tensor"),
        P(("groups", "dp"), "tensor"),
        P("dp", "tensor"),
        P("dp", "tensor"),
        P("tensor", None),
        P(None, "tensor", None),
        P(("groups", "dp")),
        P("dp", None, "tensor"),
    )
    out_specs = (P(("groups", "dp"), "tensor"), P("dp", "groups"))
    return jax.shard_map(body, mesh=mesh, in_specs=in_specs, out_specs=out_specs, check_vma=False)
```

```python
import jax
import jax.numpy as jnp
from jax import lax
from jax.experimental import pallas as pl
from jax.experimental.pallas import tpu as pltpu
from jax.sharding import PartitionSpec as P


def by_tokens(grads, weights):
    partial_grad = lax.dot_general(
        grads,
        lax.all_gather(weights, "dp", axis=0, tiled=True),
        (((1,), (1,)), ((), ())),
        preferred_element_type=jnp.float32,
    )
    return lax.psum_scatter(
        partial_grad.astype(jnp.bfloat16), "tensor", scatter_dimension=1, tiled=True
    )


def by_features(grads, weights):
    n = lax.axis_size("dp")
    partial_grad = lax.dot_general(
        lax.all_gather(grads, "dp", axis=0, tiled=True),
        weights,
        (((1,), (1,)), ((), ())),
        preferred_element_type=jnp.float32,
    )
    mine = lax.psum_scatter(
        partial_grad.astype(jnp.bfloat16), "tensor", scatter_dimension=0, tiled=True
    )
    turn = [(d * n + t, t * n + d) for d in range(n) for t in range(n)]
    return lax.ppermute(mine, ("dp", "tensor"), turn)


def plain(
    normed, grad_key, grad_value, weight_key, weight_value, proj_in, proj_out, lengths, queries
):
    grads = jnp.concatenate([grad_key, grad_value], axis=1)
    weights = jnp.concatenate([weight_key, weight_value], axis=1)
    if lax.axis_size("dp") == lax.axis_size("tensor"):
        grad_input = by_features(grads, weights)
    else:
        grad_input = by_tokens(grads, weights)
    tokens = normed.shape[0]
    rank = proj_out.shape[2]
    shards = lax.axis_size("tensor")
    own_rows = rank // shards
    in_part = jnp.dot(normed, proj_in, preferred_element_type=jnp.float32)
    out_part = jnp.stack(
        [
            jnp.dot(grad_key, proj_out[0], preferred_element_type=jnp.float32),
            jnp.dot(grad_value, proj_out[1], preferred_element_type=jnp.float32),
        ],
        axis=1,
    )
    in_whole, out_whole = (
        lax.psum(in_part.astype(jnp.bfloat16), "tensor").astype(jnp.float32),
        lax.psum(out_part.astype(jnp.bfloat16), "tensor").astype(jnp.float32),
    )
    out_own = lax.dynamic_slice_in_dim(out_whole, lax.axis_index("tensor") * own_rows, own_rows, 2)
    in_sketch = in_whole.astype(jnp.bfloat16)
    out_sketch = out_own.astype(jnp.bfloat16)
    seq_count = lengths.shape[0]
    seq_len = tokens // seq_count
    positions = lax.broadcasted_iota(jnp.int32, (seq_count, seq_len), 1)
    live = (positions < lengths[:, None]).astype(jnp.bfloat16)
    in_seq = in_sketch.reshape(seq_count, seq_len, 2, rank)
    out_seq = out_sketch.reshape(seq_count, seq_len, 2, own_rows) * live[:, :, None, None]
    sums = jnp.einsum("stla,stlb->slab", out_seq, in_seq, preferred_element_type=jnp.float32)
    scale = 1.0 / jnp.sqrt(lengths.astype(jnp.float32))
    seq_sketch = (
        (sums * scale[:, None, None, None])
        .astype(jnp.bfloat16)
        .reshape(seq_count, 2, own_rows * rank)
    )
    partial_scores = jnp.einsum(
        "qlf,slf->qs",
        queries,
        lax.all_gather(seq_sketch, "dp", axis=0, tiled=True),
        preferred_element_type=jnp.float32,
    )
    scores = lax.psum(partial_scores, "tensor") / rank
    return (grad_input, scores)


MESH = pl.DeviceIdType.MESH
F32 = jnp.float32
BF16 = jnp.bfloat16


def visit(n):
    rows = []
    for d in range(n):
        near = sorted(range(n), key=lambda j: (abs(j - d), min(j, n - 1 - j)))
        rows.append(near)
    return rows


def pick(table, d, k):
    value = jnp.int32(table[0][k])
    for place in range(1, len(table)):
        value = jnp.where(d == place, table[place][k], value)
    return value


def nt_dot(a, b):
    return lax.dot_general(a, b, (((1,), (1,)), ((), ())), preferred_element_type=F32)


def fused_kernel(
    n,
    length_ref, normed_ref, gk_ref, gv_ref, wk_ref, wv_ref, pin_ref, pout_ref, q_ref,
    out_ref, score_ref,
    grads, weights, normed, pin, pout, queries,
    acc, c_send, c_recv, x_send, x_recv, f_send, f_recv,
    sk_acc, sk_send, sk_recv, seqs, parts,
    load_sem, g_send_sem, g_recv_sem, c_sem, x_sem, f_send_sem, f_recv_sem,
    o_send_sem, o_recv_sem, sk_sem, s_send_sem, s_recv_sem, p_send_sem, p_recv_sem,
):
    group, d, t = lax.axis_index("groups"), lax.axis_index("dp"), lax.axis_index("tensor")
    core, x = lax.rem(t, 2), lax.div(t, 2)
    rows = gk_ref.shape[0]
    rank = pout_ref.shape[2]
    own_rows = rank // n
    half = wk_ref.shape[0] // 2
    quarter = half // 2
    table = visit(n)
    order = [pick(table, d, k) for k in range(n)]
    at_core = (group, d, t + 1 - 2 * core)
    at_x = (group, d, lax.rem(t + 2, 4))

    def remote(src, dst, send, recv, where):
        return pltpu.make_async_remote_copy(
            src_ref=src, dst_ref=dst, send_sem=send, recv_sem=recv,
            device_id=where, device_id_type=MESH,
        )

    loads = [
        pltpu.make_async_copy(src, dst, load_sem.at[i])
        for i, (src, dst) in enumerate(
            [
                (gk_ref, grads.at[d, 0]), (gv_ref, grads.at[d, 1]),
                (wk_ref, weights.at[0]), (wv_ref, weights.at[1]),
                (normed_ref, normed), (pin_ref, pin), (pout_ref, pout), (q_ref, queries),
            ]
        )
    ]
    for load in loads:
        load.start()

    barrier = pltpu.get_barrier_semaphore()
    for step in range(1, n):
        pl.semaphore_signal(barrier, 1, device_id=(group, lax.rem(d + step, n), t), device_id_type=MESH)
        pl.semaphore_signal(barrier, 1, device_id=(group, d, lax.rem(t + step, n)), device_id_type=MESH)
    pl.semaphore_wait(barrier, 2 * (n - 1))

    def up(j, h, src):
        return remote(src, grads.at[j, h], g_send_sem.at[0, j, h], g_recv_sem.at[j, h], (group, lax.rem(d + 1, n), t))

    def down(j, h, src):
        return remote(src, grads.at[j, h], g_send_sem.at[1, j, h], g_recv_sem.at[j, h], (group, lax.rem(d + n - 1, n), t))

    def pass_on(k, finish=False):
        j = order[k]
        for h, own in enumerate((gk_ref, gv_ref)):
            src = own if k == 0 else grads.at[j, h]
            if k > 0 and not finish:
                up(j, h, src).wait_recv()
            for copy, more in ((up, (j <= d) & (d < n - 1)), (down, (j >= d) & (d > 0))):
                @pl.when(more)
                def _(copy=copy, src=src, h=h):
                    if finish:
                        copy(j, h, src).wait_send()
                    else:
                        copy(j, h, src).start()

    def core_copy(k):
        return remote(c_send.at[k], c_recv.at[k], c_sem.at[0, k], c_sem.at[1, k], at_core)

    def x_copy(k):
        return remote(x_send.at[k], x_recv.at[k], x_sem.at[0, k], x_sem.at[1, k], at_x)

    def multiply(k):
        j = order[k]
        for sub in range(2):
            start = pl.multiple_of((1 - core) * half + sub * quarter, quarter)
            c_send[k, sub] = (
                nt_dot(grads[j, 0], weights[0, pl.ds(start, quarter), :])
                + nt_dot(grads[j, 1], weights[1, pl.ds(start, quarter), :])
            ).astype(BF16)
        core_copy(k).start()
        for sub in range(2):
            start = pl.multiple_of(core * half + sub * quarter, quarter)
            acc[k, sub] = (
                nt_dot(grads[j, 0], weights[0, pl.ds(start, quarter), :])
                + nt_dot(grads[j, 1], weights[1, pl.ds(start, quarter), :])
            )

    def add_core(k):
        core_copy(k).wait_recv()
        x_send[k] = (acc[k, 1 - x] + c_recv[k, 1 - x].astype(F32)).astype(BF16)
        x_copy(k).start()
        acc[k, x] = acc[k, x] + c_recv[k, x].astype(F32)

    def f_copy(k, source=None):
        if source is None:
            return remote(f_send.at[k], f_recv.at[d], f_send_sem.at[k], f_recv_sem.at[d], (group, order[k], t))
        return remote(f_send.at[k], f_recv.at[source], f_send_sem.at[k], f_recv_sem.at[source], (group, order[k], t))

    def add_x(k):
        x_copy(k).wait_recv()
        total = (acc[k, x] + x_recv[k].astype(F32)).astype(BF16)
        if k == 0:
            f_recv[d] = total
        else:
            f_send[k] = total
            f_copy(k).start()

    columns = pl.ds(pl.multiple_of(core * half + x * quarter, quarter), quarter)

    def deliver(k, finish=False):
        source = order[k]
        if k > 0 and not finish:
            f_copy(k, source).wait_recv()

        @pl.when(source == t)
        def _():
            if not finish:
                pltpu.make_async_copy(f_recv.at[source], out_ref.at[:, columns], o_recv_sem.at[t]).start()

        @pl.when(source != t)
        def _():
            copy = remote(
                f_recv.at[source], out_ref.at[:, columns], o_send_sem.at[k], o_recv_sem.at[t], (group, d, source)
            )
            if finish:
                copy.wait_send()
            else:
                copy.start()

    def sk_copy(i, where):
        return remote(sk_send.at[i], sk_recv.at[i], sk_sem.at[0, i], sk_sem.at[1, i], where)

    def sketch_parts():
        for load in loads[4:7]:
            load.wait()
        sk_acc[:, : 2 * rank] = jnp.dot(normed[...], pin[...], preferred_element_type=F32)
        sk_acc[:, 2 * rank :] = jnp.concatenate(
            [
                jnp.dot(grads[d, 0], pout[0], preferred_element_type=F32),
                jnp.dot(grads[d, 1], pout[1], preferred_element_type=F32),
            ],
            axis=1,
        )
        sk_send[0] = sk_acc[...].astype(BF16)
        sk_copy(0, at_core).start()

    def sketch_x():
        sk_copy(0, at_core).wait_recv()
        sk_acc[...] = sk_acc[...] + sk_recv[0].astype(F32)
        sk_send[1] = sk_acc[...].astype(BF16)
        sk_copy(1, at_x).start()

    def seq_copy(step, source=None):
        slot = d if source is None else source
        return remote(
            seqs.at[slot], seqs.at[slot], s_send_sem.at[step], s_recv_sem.at[slot],
            (group, lax.rem(d + step, n), t),
        )

    def sketch_seq():
        sk_copy(1, at_x).wait_recv()
        whole = (sk_acc[...] + sk_recv[1].astype(F32)).astype(BF16)
        length = length_ref[0]
        live = lax.broadcasted_iota(jnp.int32, (rows, 2 * rank), 0) < length
        outs = jnp.where(live, whole[:, 2 * rank :].astype(F32), 0.0).astype(BF16)
        c = lax.broadcasted_iota(jnp.int32, (2 * rank, 2 * own_rows), 0)
        r = lax.broadcasted_iota(jnp.int32, (2 * rank, 2 * own_rows), 1)
        chosen = (r // own_rows) * rank + t * own_rows + lax.rem(r, own_rows)
        mine = jnp.dot(outs, (c == chosen).astype(F32).astype(BF16), preferred_element_type=F32).astype(BF16)
        sums = lax.dot_general(
            mine, whole[:, : 2 * rank], (((0,), (0,)), ((), ())), preferred_element_type=F32
        )
        scale = 1.0 / jnp.sqrt(jnp.full(sums.shape, length, jnp.int32).astype(F32))
        seqs[d] = (sums * scale).astype(BF16)
        for step in range(1, n):
            seq_copy(step).start()

    def part_copy(step, source=None):
        slot = t if source is None else source
        return remote(
            parts.at[slot], parts.at[slot], p_send_sem.at[step], p_recv_sem.at[slot],
            (group, d, lax.rem(t + step, n)),
        )

    def part_scores():
        for step in range(1, n):
            seq_copy(step, lax.rem(d + step, n)).wait_recv()
        loads[7].wait()
        wide = 2 * own_rows * rank
        block = 2 * own_rows
        f = lax.broadcasted_iota(jnp.int32, (2 * rank, wide), 1)
        c = lax.broadcasted_iota(jnp.int32, (2 * rank, wide), 0)
        spread = (c == (f // (own_rows * rank)) * rank + lax.rem(f, rank)).astype(F32).astype(BF16)
        everything = jnp.concatenate([seqs[i] for i in range(n)], axis=0)
        tall = jnp.dot(everything, spread, preferred_element_type=F32)
        f = lax.broadcasted_iota(jnp.int32, (n * block, wide), 1)
        r = lax.broadcasted_iota(jnp.int32, (n * block, wide), 0)
        kept = jnp.where(lax.rem(r, block) == f // rank, tall, 0.0).astype(BF16)
        s = lax.broadcasted_iota(jnp.int32, (8, n * block), 0)
        r = lax.broadcasted_iota(jnp.int32, (8, n * block), 1)
        flat = jnp.dot((r // block == s).astype(F32).astype(BF16), kept, preferred_element_type=F32).astype(BF16)
        parts[t] = nt_dot(flat, queries[...])
        for step in range(1, n):
            part_copy(step).start()

    def whole_scores():
        for step in range(1, n):
            part_copy(step, lax.rem(t + step, n)).wait_recv()
        total = parts[0]
        for i in range(1, n):
            total = total + parts[i]
        score_ref[...] = total * (1.0 / rank)

    pass_on(0)
    for load in loads[:4]:
        load.wait()
    multiply(0)
    sketch_parts()
    add_core(0)
    sketch_x()
    pass_on(1)
    multiply(1)
    add_x(0)
    deliver(0)
    pass_on(2)
    add_core(1)
    multiply(2)
    sketch_seq()
    add_x(1)
    add_core(2)
    pass_on(3)
    multiply(3)
    add_x(2)
    add_core(3)
    part_scores()
    deliver(1)
    add_x(3)
    deliver(2)
    deliver(3)
    whole_scores()
    for source in range(n):
        remote(f_recv.at[0], out_ref.at[:, pl.ds(((source % 2) * 2 + source // 2) * quarter, quarter)],
               o_send_sem.at[0], o_recv_sem.at[source], at_core).wait_recv()
    for k in range(n):
        pass_on(k, finish=True)
        core_copy(k).wait_send()
        x_copy(k).wait_send()
        if k > 0:
            f_copy(k).wait_send()
            seq_copy(k).wait_send()
            part_copy(k).wait_send()
        deliver(k, finish=True)
    sk_copy(0, at_core).wait_send()
    sk_copy(1, at_x).wait_send()


def body(
    normed, grad_key, grad_value, weight_key, weight_value, proj_in, proj_out, lengths, queries
):
    n = lax.axis_size("dp")
    rows, wide = normed.shape
    depth = grad_key.shape[1]
    rank = proj_out.shape[2]
    count = queries.shape[0]
    features = weight_key.shape[0]
    if not (n == lax.axis_size("tensor") == 4 and lengths.shape[0] == 1 and features == wide):
        return plain(
            normed, grad_key, grad_value, weight_key, weight_value, proj_in, proj_out, lengths, queries
        )
    quarter = features // 4
    flat_queries = queries.reshape(count, -1)
    anywhere = pl.BlockSpec(memory_space=pl.ANY)
    dma = pltpu.SemaphoreType.DMA
    grad_input, scores = pl.pallas_call(
        lambda *refs: fused_kernel(n, *refs),
        out_shape=(
            jax.ShapeDtypeStruct((rows, wide), BF16),
            jax.ShapeDtypeStruct((8, count), F32),
        ),
        in_specs=[pl.BlockSpec(memory_space=pltpu.SMEM)] + [anywhere] * 8,
        out_specs=(anywhere, pl.BlockSpec(memory_space=pltpu.VMEM)),
        scratch_shapes=[
            pltpu.VMEM((n, 2, rows, depth), BF16),
            pltpu.VMEM((2, features, depth), BF16),
            pltpu.VMEM(normed.shape, BF16),
            pltpu.VMEM(proj_in.shape, BF16),
            pltpu.VMEM(proj_out.shape, BF16),
            pltpu.VMEM(flat_queries.shape, BF16),
            pltpu.VMEM((n, 2, rows, quarter), F32),
            pltpu.VMEM((n, 2, rows, quarter), BF16),
            pltpu.VMEM((n, 2, rows, quarter), BF16),
            pltpu.VMEM((n, rows, quarter), BF16),
            pltpu.VMEM((n, rows, quarter), BF16),
            pltpu.VMEM((n, rows, quarter), BF16),
            pltpu.VMEM((n, rows, quarter), BF16),
            pltpu.VMEM((rows, 4 * rank), F32),
            pltpu.VMEM((2, rows, 4 * rank), BF16),
            pltpu.VMEM((2, rows, 4 * rank), BF16),
            pltpu.VMEM((n, 2 * rank // n, 2 * rank), BF16),
            pltpu.VMEM((n, 8, count), F32),
            dma((8,)),
            dma((2, n, 2)),
            dma((n, 2)),
            dma((2, n)),
            dma((2, n)),
            dma((n,)),
            dma((n,)),
            dma((n,)),
            dma((n,)),
            dma((2, 2)),
            dma((n,)),
            dma((n,)),
            dma((n,)),
            dma((n,)),
        ],
        compiler_params=pltpu.CompilerParams(
            collective_id=0, has_side_effects=True, vmem_limit_bytes=48 * 1024 * 1024
        ),
    )(
        lengths, normed, grad_key, grad_value, weight_key, weight_value, proj_in, proj_out, flat_queries
    )
    return (grad_input, scores[:n].T)


def solution(mesh):
    in_specs = (
        P(("groups", "dp"), "tensor"),
        P(("groups", "dp"), "tensor"),
        P(("groups", "dp"), "tensor"),
        P("dp", "tensor"),
        P("dp", "tensor"),
        P("tensor", None),
        P(None, "tensor", None),
        P(("groups", "dp")),
        P("dp", None, "tensor"),
    )
    out_specs = (P(("groups", "dp"), "tensor"), P("dp", "groups"))
    return jax.shard_map(body, mesh=mesh, in_specs=in_specs, out_specs=out_specs, check_vma=False)
```

```python
import jax
import jax.numpy as jnp
from jax import lax
from jax.experimental import pallas as pl
from jax.experimental.pallas import tpu as pltpu
from jax.sharding import PartitionSpec as P


def by_tokens(grads, weights):
    partial_grad = lax.dot_general(
        grads,
        lax.all_gather(weights, "dp", axis=0, tiled=True),
        (((1,), (1,)), ((), ())),
        preferred_element_type=jnp.float32,
    )
    return lax.psum_scatter(
        partial_grad.astype(jnp.bfloat16), "tensor", scatter_dimension=1, tiled=True
    )


def by_features(grads, weights):
    n = lax.axis_size("dp")
    partial_grad = lax.dot_general(
        lax.all_gather(grads, "dp", axis=0, tiled=True),
        weights,
        (((1,), (1,)), ((), ())),
        preferred_element_type=jnp.float32,
    )
    mine = lax.psum_scatter(
        partial_grad.astype(jnp.bfloat16), "tensor", scatter_dimension=0, tiled=True
    )
    turn = [(d * n + t, t * n + d) for d in range(n) for t in range(n)]
    return lax.ppermute(mine, ("dp", "tensor"), turn)


def plain(
    normed, grad_key, grad_value, weight_key, weight_value, proj_in, proj_out, lengths, queries
):
    grads = jnp.concatenate([grad_key, grad_value], axis=1)
    weights = jnp.concatenate([weight_key, weight_value], axis=1)
    if lax.axis_size("dp") == lax.axis_size("tensor"):
        grad_input = by_features(grads, weights)
    else:
        grad_input = by_tokens(grads, weights)
    tokens = normed.shape[0]
    rank = proj_out.shape[2]
    shards = lax.axis_size("tensor")
    own_rows = rank // shards
    in_part = jnp.dot(normed, proj_in, preferred_element_type=jnp.float32)
    out_part = jnp.stack(
        [
            jnp.dot(grad_key, proj_out[0], preferred_element_type=jnp.float32),
            jnp.dot(grad_value, proj_out[1], preferred_element_type=jnp.float32),
        ],
        axis=1,
    )
    in_whole, out_whole = (
        lax.psum(in_part.astype(jnp.bfloat16), "tensor").astype(jnp.float32),
        lax.psum(out_part.astype(jnp.bfloat16), "tensor").astype(jnp.float32),
    )
    out_own = lax.dynamic_slice_in_dim(out_whole, lax.axis_index("tensor") * own_rows, own_rows, 2)
    in_sketch = in_whole.astype(jnp.bfloat16)
    out_sketch = out_own.astype(jnp.bfloat16)
    seq_count = lengths.shape[0]
    seq_len = tokens // seq_count
    positions = lax.broadcasted_iota(jnp.int32, (seq_count, seq_len), 1)
    live = (positions < lengths[:, None]).astype(jnp.bfloat16)
    in_seq = in_sketch.reshape(seq_count, seq_len, 2, rank)
    out_seq = out_sketch.reshape(seq_count, seq_len, 2, own_rows) * live[:, :, None, None]
    sums = jnp.einsum("stla,stlb->slab", out_seq, in_seq, preferred_element_type=jnp.float32)
    scale = 1.0 / jnp.sqrt(lengths.astype(jnp.float32))
    seq_sketch = (
        (sums * scale[:, None, None, None])
        .astype(jnp.bfloat16)
        .reshape(seq_count, 2, own_rows * rank)
    )
    partial_scores = jnp.einsum(
        "qlf,slf->qs",
        queries,
        lax.all_gather(seq_sketch, "dp", axis=0, tiled=True),
        preferred_element_type=jnp.float32,
    )
    scores = lax.psum(partial_scores, "tensor") / rank
    return (grad_input, scores)


MESH = pl.DeviceIdType.MESH
F32 = jnp.float32
BF16 = jnp.bfloat16


CUTS = 2


def visit(n):
    rows = []
    for d in range(n):
        far = [(j, h) for h in range(CUTS) for j in range(n) if j != d]
        far.sort(key=lambda item: ((abs(item[0] - d) - 1) * CUTS + item[1], min(item[0], n - 1 - item[0])))
        rows.append([(d, 0)] + far + [(d, h) for h in range(1, CUTS)])
    return rows


def arrivals(n):
    table = visit(n)
    rows = []
    for i in range(n):
        far = [(s, h) for s in range(n) if s != i for h in range(CUTS)]
        far.sort(key=lambda item: (table[item[0]].index((i, item[1])), abs(item[0] - i)))
        rows.append(far)
    return rows


def pick(table, d, k):
    values = []
    for part in range(2):
        value = jnp.int32(table[0][k][part])
        for place in range(1, len(table)):
            value = jnp.where(d == place, table[place][k][part], value)
        values.append(value)
    return values


def nt_dot(a, b):
    return lax.dot_general(a, b, (((1,), (1,)), ((), ())), preferred_element_type=F32)


def fused_kernel(
    n,
    length_ref, normed_ref, gk_ref, gv_ref, wk_ref, wv_ref, pin_ref, pout_ref, q_ref,
    out_ref, score_ref,
    grads, weights, normed, pin, pout, queries,
    acc, c_send, c_recv, x_send, x_recv, f_send, f_recv,
    sk_acc, sk_send, sk_recv, seqs, parts,
    load_sem, g_send_sem, g_recv_sem, c_sem, x_sem, f_send_sem, f_recv_sem,
    o_send_sem, o_recv_sem, sk_sem, s_send_sem, s_recv_sem, p_send_sem, p_recv_sem,
):
    group, d, t = lax.axis_index("groups"), lax.axis_index("dp"), lax.axis_index("tensor")
    core, x = lax.rem(t, 2), lax.div(t, 2)
    rows = gk_ref.shape[0]
    rank = pout_ref.shape[1]
    own_rows = rank // n
    half = wk_ref.shape[0] // 2
    quarter = half // 2
    table = visit(n)
    items = n * CUTS
    order = [pick(table, d, k) for k in range(items)]
    coming = arrivals(n)
    expected = [pick(coming, d, k) for k in range(items - CUTS)]
    cut = rows // CUTS
    at_core = (group, d, t + 1 - 2 * core)
    at_x = (group, d, lax.rem(t + 2, 4))

    def remote(src, dst, send, recv, where):
        return pltpu.make_async_remote_copy(
            src_ref=src, dst_ref=dst, send_sem=send, recv_sem=recv,
            device_id=where, device_id_type=MESH,
        )

    loads = [
        pltpu.make_async_copy(src, dst, load_sem.at[i])
        for i, (src, dst) in enumerate(
            [(src.at[pl.ds(h * cut, cut)], grads.at[d, h, v]) for v, src in enumerate((gk_ref, gv_ref)) for h in range(CUTS)]
            + [
                (wk_ref, weights.at[0]), (wv_ref, weights.at[1]),
                (normed_ref, normed), (pin_ref, pin), (pout_ref, pout), (q_ref, queries),
            ]
        )
    ]
    for load in loads:
        load.start()

    barrier = pltpu.get_barrier_semaphore()
    for step in range(1, n):
        pl.semaphore_signal(barrier, 1, device_id=(group, lax.rem(d + step, n), t), device_id_type=MESH)
        pl.semaphore_signal(barrier, 1, device_id=(group, d, lax.rem(t + step, n)), device_id_type=MESH)
    pl.semaphore_wait(barrier, 2 * (n - 1))

    def up(j, h, v, src):
        return remote(
            src, grads.at[j, h, v], g_send_sem.at[0, j, h, v], g_recv_sem.at[j, h, v], (group, lax.rem(d + 1, n), t)
        )

    def down(j, h, v, src):
        return remote(
            src, grads.at[j, h, v], g_send_sem.at[1, j, h, v], g_recv_sem.at[j, h, v], (group, lax.rem(d + n - 1, n), t)
        )

    def pass_on(k, finish=False):
        own = k == 0 or k > items - CUTS
        j, h = order[k]
        for v, ref in enumerate((gk_ref, gv_ref)):
            src = ref.at[pl.ds((0 if k == 0 else k - items + CUTS) * cut, cut)] if own else grads.at[j, h, v]
            if not own and not finish:
                up(j, h, v, src).wait_recv()
            for copy, more in ((up, (j <= d) & (d < n - 1)), (down, (j >= d) & (d > 0))):
                @pl.when(more)
                def _(copy=copy, src=src, v=v):
                    if finish:
                        copy(j, h, v, src).wait_send()
                    else:
                        copy(j, h, v, src).start()

    def core_copy(k):
        return remote(c_send.at[k], c_recv.at[k], c_sem.at[0, k], c_sem.at[1, k], at_core)

    def x_copy(k):
        return remote(x_send.at[k], x_recv.at[k], x_sem.at[0, k], x_sem.at[1, k], at_x)

    def multiply(k):
        j, h = order[k]
        for sub in range(2):
            start = pl.multiple_of((1 - core) * half + sub * quarter, quarter)
            c_send[k, sub] = (
                nt_dot(grads[j, h, 0], weights[0, pl.ds(start, quarter), :])
                + nt_dot(grads[j, h, 1], weights[1, pl.ds(start, quarter), :])
            ).astype(BF16)
        core_copy(k).start()
        for sub in range(2):
            start = pl.multiple_of(core * half + sub * quarter, quarter)
            acc[k, sub] = (
                nt_dot(grads[j, h, 0], weights[0, pl.ds(start, quarter), :])
                + nt_dot(grads[j, h, 1], weights[1, pl.ds(start, quarter), :])
            )

    def add_core(k):
        core_copy(k).wait_recv()
        x_send[k] = (acc[k, 1 - x] + c_recv[k, 1 - x].astype(F32)).astype(BF16)
        x_copy(k).start()
        acc[k, x] = acc[k, x] + c_recv[k, x].astype(F32)

    def f_copy(k):
        i, h = order[k]
        return remote(f_send.at[k], f_recv.at[d, h], f_send_sem.at[k], f_recv_sem.at[d, h], (group, i, t))

    def add_x(k):
        x_copy(k).wait_recv()
        total = (acc[k, x] + x_recv[k].astype(F32)).astype(BF16)
        if k == 0 or k > items - CUTS:
            f_recv[d, 0 if k == 0 else k - items + CUTS] = total
        else:
            f_send[k] = total
            f_copy(k).start()

    columns = pl.ds(pl.multiple_of(core * half + x * quarter, quarter), quarter)

    def deliver(source, h, own=False, finish=False):
        if not own and not finish:
            remote(
                f_send.at[0], f_recv.at[source, h], f_send_sem.at[0], f_recv_sem.at[source, h], (group, source, t)
            ).wait_recv()
        there = out_ref.at[pl.ds(pl.multiple_of(h * cut, cut), cut), columns]

        @pl.when(source == t)
        def _():
            if not finish:
                pltpu.make_async_copy(f_recv.at[source, h], there, o_recv_sem.at[t, h]).start()

        @pl.when(source != t)
        def _():
            copy = remote(
                f_recv.at[source, h], there, o_send_sem.at[source, h], o_recv_sem.at[t, h], (group, d, source)
            )
            if finish:
                copy.wait_send()
            else:
                copy.start()

    def sk_copy(i, where):
        return remote(sk_send.at[i], sk_recv.at[i], sk_sem.at[0, i], sk_sem.at[1, i], where)

    def sketch_parts():
        for load in loads[6:9]:
            load.wait()
        sk_acc[:, : 2 * rank] = jnp.dot(normed[...], pin[...], preferred_element_type=F32)
        for h in range(CUTS):
            sk_acc[pl.ds(h * cut, cut), 2 * rank :] = jnp.concatenate(
                [nt_dot(grads[d, h, 0], pout[0]), nt_dot(grads[d, h, 1], pout[1])], axis=1
            )
        sk_send[0] = sk_acc[...].astype(BF16)
        sk_copy(0, at_core).start()

    def sketch_x():
        sk_copy(0, at_core).wait_recv()
        sk_acc[...] = sk_acc[...] + sk_recv[0].astype(F32)
        sk_send[1] = sk_acc[...].astype(BF16)
        sk_copy(1, at_x).start()

    def seq_copy(step, source=None):
        slot = d if source is None else source
        return remote(
            seqs.at[slot], seqs.at[slot], s_send_sem.at[step], s_recv_sem.at[slot],
            (group, lax.rem(d + step, n), t),
        )

    def sketch_seq():
        sk_copy(1, at_x).wait_recv()
        whole = (sk_acc[...] + sk_recv[1].astype(F32)).astype(BF16)
        length = length_ref[0]
        live = lax.broadcasted_iota(jnp.int32, (rows, 2 * rank), 0) < length
        outs = jnp.where(live, whole[:, 2 * rank :].astype(F32), 0.0).astype(BF16)
        c = lax.broadcasted_iota(jnp.int32, (2 * rank, 2 * own_rows), 0)
        r = lax.broadcasted_iota(jnp.int32, (2 * rank, 2 * own_rows), 1)
        chosen = (r // own_rows) * rank + t * own_rows + lax.rem(r, own_rows)
        mine = jnp.dot(outs, (c == chosen).astype(F32).astype(BF16), preferred_element_type=F32).astype(BF16)
        sums = lax.dot_general(
            mine, whole[:, : 2 * rank], (((0,), (0,)), ((), ())), preferred_element_type=F32
        )
        scale = 1.0 / jnp.sqrt(jnp.full(sums.shape, length, jnp.int32).astype(F32))
        seqs[d] = (sums * scale).astype(BF16)
        for step in range(1, n):
            seq_copy(step).start()

    def part_copy(step, source=None):
        slot = t if source is None else source
        return remote(
            parts.at[slot], parts.at[slot], p_send_sem.at[step], p_recv_sem.at[slot],
            (group, d, lax.rem(t + step, n)),
        )

    def part_scores():
        for step in range(1, n):
            seq_copy(step, lax.rem(d + step, n)).wait_recv()
        loads[9].wait()
        wide = 2 * own_rows * rank
        block = 2 * own_rows
        f = lax.broadcasted_iota(jnp.int32, (2 * rank, wide), 1)
        c = lax.broadcasted_iota(jnp.int32, (2 * rank, wide), 0)
        spread = (c == (f // (own_rows * rank)) * rank + lax.rem(f, rank)).astype(F32).astype(BF16)
        everything = jnp.concatenate([seqs[i] for i in range(n)], axis=0)
        tall = jnp.dot(everything, spread, preferred_element_type=F32)
        f = lax.broadcasted_iota(jnp.int32, (n * block, wide), 1)
        r = lax.broadcasted_iota(jnp.int32, (n * block, wide), 0)
        kept = jnp.where(lax.rem(r, block) == f // rank, tall, 0.0).astype(BF16)
        s = lax.broadcasted_iota(jnp.int32, (8, n * block), 0)
        r = lax.broadcasted_iota(jnp.int32, (8, n * block), 1)
        flat = jnp.dot((r // block == s).astype(F32).astype(BF16), kept, preferred_element_type=F32).astype(BF16)
        parts[t] = nt_dot(flat, queries[...])
        for step in range(1, n):
            part_copy(step).start()

    def whole_scores():
        for step in range(1, n):
            part_copy(step, lax.rem(t + step, n)).wait_recv()
        total = parts[0]
        for i in range(1, n):
            total = total + parts[i]
        score_ref[...] = total * (1.0 / rank)

    pass_on(0)
    for h in range(1, CUTS):
        pass_on(items - CUTS + h)
    for load in loads[:6]:
        load.wait()
    multiply(0)
    pass_on(1)
    add_core(0)
    multiply(1)
    pass_on(2)
    sketch_parts()
    add_core(1)
    multiply(2)
    pass_on(3)
    sketch_x()
    add_core(2)
    multiply(3)
    add_x(0)
    pass_on(4)
    add_core(3)
    add_x(1)
    multiply(4)
    pass_on(5)
    add_core(4)
    multiply(5)
    sketch_seq()
    add_x(2)
    pass_on(6)
    add_core(5)
    multiply(6)
    add_x(3)
    add_core(6)
    multiply(7)
    add_core(7)
    deliver(d, 0, own=True)
    part_scores()
    add_x(4)
    deliver(*expected[0])
    deliver(*expected[1])
    add_x(5)
    add_x(6)
    deliver(*expected[2])
    deliver(*expected[3])
    add_x(7)
    deliver(d, 1, own=True)
    deliver(*expected[4])
    deliver(*expected[5])
    whole_scores()
    for source in range(n):
        for h in range(CUTS):
            place = pl.ds(((source % 2) * 2 + source // 2) * quarter, quarter)
            remote(f_recv.at[0, h], out_ref.at[pl.ds(h * cut, cut), place],
                   o_send_sem.at[0, 0], o_recv_sem.at[source, h], at_core).wait_recv()
    for k in range(items):
        pass_on(k, finish=True)
        core_copy(k).wait_send()
        x_copy(k).wait_send()
        if 0 < k <= items - CUTS:
            f_copy(k).wait_send()
    for k in range(1, n):
        seq_copy(k).wait_send()
        part_copy(k).wait_send()
    for source in range(n):
        for h in range(CUTS):
            deliver(source, h, finish=True)
    sk_copy(0, at_core).wait_send()
    sk_copy(1, at_x).wait_send()


def body(
    normed, grad_key, grad_value, weight_key, weight_value, proj_in, proj_out, lengths, queries
):
    n = lax.axis_size("dp")
    rows, wide = normed.shape
    depth = grad_key.shape[1]
    rank = proj_out.shape[2]
    count = queries.shape[0]
    features = weight_key.shape[0]
    if not (n == lax.axis_size("tensor") == 4 and lengths.shape[0] == 1 and features == wide):
        return plain(
            normed, grad_key, grad_value, weight_key, weight_value, proj_in, proj_out, lengths, queries
        )
    quarter = features // 4
    items, cut = n * CUTS, rows // CUTS
    flat_queries = queries.reshape(count, -1)
    anywhere = pl.BlockSpec(memory_space=pl.ANY)
    dma = pltpu.SemaphoreType.DMA
    grad_input, scores = pl.pallas_call(
        lambda *refs: fused_kernel(n, *refs),
        out_shape=(
            jax.ShapeDtypeStruct((rows, wide), BF16),
            jax.ShapeDtypeStruct((8, count), F32),
        ),
        in_specs=[pl.BlockSpec(memory_space=pltpu.SMEM)] + [anywhere] * 8,
        out_specs=(anywhere, pl.BlockSpec(memory_space=pltpu.VMEM)),
        scratch_shapes=[
            pltpu.VMEM((n, CUTS, 2, cut, depth), BF16),
            pltpu.VMEM((2, features, depth), BF16),
            pltpu.VMEM(normed.shape, BF16),
            pltpu.VMEM(proj_in.shape, BF16),
            pltpu.VMEM((2, rank, depth), BF16),
            pltpu.VMEM(flat_queries.shape, BF16),
            pltpu.VMEM((items, 2, cut, quarter), F32),
            pltpu.VMEM((items, 2, cut, quarter), BF16),
            pltpu.VMEM((items, 2, cut, quarter), BF16),
            pltpu.VMEM((items, cut, quarter), BF16),
            pltpu.VMEM((items, cut, quarter), BF16),
            pltpu.VMEM((items, cut, quarter), BF16),
            pltpu.VMEM((n, CUTS, cut, quarter), BF16),
            pltpu.VMEM((rows, 4 * rank), F32),
            pltpu.VMEM((2, rows, 4 * rank), BF16),
            pltpu.VMEM((2, rows, 4 * rank), BF16),
            pltpu.VMEM((n, 2 * rank // n, 2 * rank), BF16),
            pltpu.VMEM((n, 8, count), F32),
            dma((10,)),
            dma((2, n, CUTS, 2)),
            dma((n, CUTS, 2)),
            dma((2, items)),
            dma((2, items)),
            dma((items,)),
            dma((n, CUTS)),
            dma((n, CUTS)),
            dma((n, CUTS)),
            dma((2, 2)),
            dma((n,)),
            dma((n,)),
            dma((n,)),
            dma((n,)),
        ],
        compiler_params=pltpu.CompilerParams(
            collective_id=0, has_side_effects=True, vmem_limit_bytes=62 * 1024 * 1024
        ),
    )(
        lengths, normed, grad_key, grad_value, weight_key, weight_value, proj_in,
        jnp.swapaxes(proj_out, 1, 2), flat_queries,
    )
    return (grad_input, scores[:n].T)


def solution(mesh):
    in_specs = (
        P(("groups", "dp"), "tensor"),
        P(("groups", "dp"), "tensor"),
        P(("groups", "dp"), "tensor"),
        P("dp", "tensor"),
        P("dp", "tensor"),
        P("tensor", None),
        P(None, "tensor", None),
        P(("groups", "dp")),
        P("dp", None, "tensor"),
    )
    out_specs = (P(("groups", "dp"), "tensor"), P("dp", "groups"))
    return jax.shard_map(body, mesh=mesh, in_specs=in_specs, out_specs=out_specs, check_vma=False)
```

```python
import jax
import jax.numpy as jnp
from jax import lax
from jax.experimental import pallas as pl
from jax.experimental.pallas import tpu as pltpu
from jax.sharding import PartitionSpec as P


def by_tokens(grads, weights):
    partial_grad = lax.dot_general(
        grads,
        lax.all_gather(weights, "dp", axis=0, tiled=True),
        (((1,), (1,)), ((), ())),
        preferred_element_type=jnp.float32,
    )
    return lax.psum_scatter(
        partial_grad.astype(jnp.bfloat16), "tensor", scatter_dimension=1, tiled=True
    )


def by_features(grads, weights):
    n = lax.axis_size("dp")
    partial_grad = lax.dot_general(
        lax.all_gather(grads, "dp", axis=0, tiled=True),
        weights,
        (((1,), (1,)), ((), ())),
        preferred_element_type=jnp.float32,
    )
    mine = lax.psum_scatter(
        partial_grad.astype(jnp.bfloat16), "tensor", scatter_dimension=0, tiled=True
    )
    turn = [(d * n + t, t * n + d) for d in range(n) for t in range(n)]
    return lax.ppermute(mine, ("dp", "tensor"), turn)


def plain(
    normed, grad_key, grad_value, weight_key, weight_value, proj_in, proj_out, lengths, queries
):
    grads = jnp.concatenate([grad_key, grad_value], axis=1)
    weights = jnp.concatenate([weight_key, weight_value], axis=1)
    if lax.axis_size("dp") == lax.axis_size("tensor"):
        grad_input = by_features(grads, weights)
    else:
        grad_input = by_tokens(grads, weights)
    tokens = normed.shape[0]
    rank = proj_out.shape[2]
    shards = lax.axis_size("tensor")
    own_rows = rank // shards
    in_part = jnp.dot(normed, proj_in, preferred_element_type=jnp.float32)
    out_part = jnp.stack(
        [
            jnp.dot(grad_key, proj_out[0], preferred_element_type=jnp.float32),
            jnp.dot(grad_value, proj_out[1], preferred_element_type=jnp.float32),
        ],
        axis=1,
    )
    in_whole, out_whole = (
        lax.psum(in_part.astype(jnp.bfloat16), "tensor").astype(jnp.float32),
        lax.psum(out_part.astype(jnp.bfloat16), "tensor").astype(jnp.float32),
    )
    out_own = lax.dynamic_slice_in_dim(out_whole, lax.axis_index("tensor") * own_rows, own_rows, 2)
    in_sketch = in_whole.astype(jnp.bfloat16)
    out_sketch = out_own.astype(jnp.bfloat16)
    seq_count = lengths.shape[0]
    seq_len = tokens // seq_count
    positions = lax.broadcasted_iota(jnp.int32, (seq_count, seq_len), 1)
    live = (positions < lengths[:, None]).astype(jnp.bfloat16)
    in_seq = in_sketch.reshape(seq_count, seq_len, 2, rank)
    out_seq = out_sketch.reshape(seq_count, seq_len, 2, own_rows) * live[:, :, None, None]
    sums = jnp.einsum("stla,stlb->slab", out_seq, in_seq, preferred_element_type=jnp.float32)
    scale = 1.0 / jnp.sqrt(lengths.astype(jnp.float32))
    seq_sketch = (
        (sums * scale[:, None, None, None])
        .astype(jnp.bfloat16)
        .reshape(seq_count, 2, own_rows * rank)
    )
    partial_scores = jnp.einsum(
        "qlf,slf->qs",
        queries,
        lax.all_gather(seq_sketch, "dp", axis=0, tiled=True),
        preferred_element_type=jnp.float32,
    )
    scores = lax.psum(partial_scores, "tensor") / rank
    return (grad_input, scores)


MESH = pl.DeviceIdType.MESH
F32 = jnp.float32
BF16 = jnp.bfloat16


CUTS = 2


def visit(n):
    rows = []
    for d in range(n):
        far = [(j, h) for h in range(CUTS) for j in range(n) if j != d]
        far.sort(key=lambda item: ((abs(item[0] - d) - 1) * CUTS + item[1], min(item[0], n - 1 - item[0])))
        rows.append([(d, 0)] + far + [(d, h) for h in range(1, CUTS)])
    return rows


def arrivals(n):
    table = visit(n)
    rows = []
    for i in range(n):
        far = [(s, h) for s in range(n) if s != i for h in range(CUTS)]
        far.sort(key=lambda item: (table[item[0]].index((i, item[1])), abs(item[0] - i)))
        rows.append(far)
    return rows


def pick(table, d, k):
    values = []
    for part in range(2):
        value = jnp.int32(table[0][k][part])
        for place in range(1, len(table)):
            value = jnp.where(d == place, table[place][k][part], value)
        values.append(value)
    return values


def nt_dot(a, b):
    return lax.dot_general(a, b, (((1,), (1,)), ((), ())), preferred_element_type=F32)


def fused_kernel(
    n,
    length_ref, normed_ref, gk_ref, gv_ref, wk_ref, wv_ref, pin_ref, pout_ref, q_ref,
    out_ref, score_ref,
    grads, weights, normed, pin, pout, queries,
    acc, c_send, c_recv, x_send, x_recv, f_send, f_recv,
    sk_acc, sk_send, sk_recv, seqs, parts,
    load_sem, g_send_sem, g_recv_sem, c_sem, x_sem, f_send_sem, f_recv_sem,
    o_send_sem, o_recv_sem, sk_sem, s_send_sem, s_recv_sem, p_send_sem, p_recv_sem,
):
    group, d, t = lax.axis_index("groups"), lax.axis_index("dp"), lax.axis_index("tensor")
    core, x = lax.rem(t, 2), lax.div(t, 2)
    rows = gk_ref.shape[0]
    rank = pout_ref.shape[1]
    own_rows = rank // n
    half = wk_ref.shape[0] // 2
    quarter = half // 2
    table = visit(n)
    items = n * CUTS
    order = [pick(table, d, k) for k in range(items)]
    coming = arrivals(n)
    expected = [pick(coming, d, k) for k in range(items - CUTS)]
    cut = rows // CUTS
    at_core = (group, d, t + 1 - 2 * core)
    at_x = (group, d, lax.rem(t + 2, 4))

    def remote(src, dst, send, recv, where):
        return pltpu.make_async_remote_copy(
            src_ref=src, dst_ref=dst, send_sem=send, recv_sem=recv,
            device_id=where, device_id_type=MESH,
        )

    loads = [
        pltpu.make_async_copy(src, dst, load_sem.at[i])
        for i, (src, dst) in enumerate(
            [(src.at[pl.ds(h * cut, cut)], grads.at[d, h, v]) for v, src in enumerate((gk_ref, gv_ref)) for h in range(CUTS)]
            + [
                (wk_ref, weights.at[0]), (wv_ref, weights.at[1]),
                (normed_ref, normed), (pin_ref, pin), (pout_ref, pout), (q_ref, queries),
            ]
        )
    ]
    for load in loads:
        load.start()

    barrier = pltpu.get_barrier_semaphore()
    for step in range(1, n):
        pl.semaphore_signal(barrier, 1, device_id=(group, lax.rem(d + step, n), t), device_id_type=MESH)
        pl.semaphore_signal(barrier, 1, device_id=(group, d, lax.rem(t + step, n)), device_id_type=MESH)
    pl.semaphore_wait(barrier, 2 * (n - 1))

    def up(j, h, v, src):
        return remote(
            src, grads.at[j, h, v], g_send_sem.at[0, j, h, v], g_recv_sem.at[j, h, v], (group, lax.rem(d + 1, n), t)
        )

    def down(j, h, v, src):
        return remote(
            src, grads.at[j, h, v], g_send_sem.at[1, j, h, v], g_recv_sem.at[j, h, v], (group, lax.rem(d + n - 1, n), t)
        )

    def pass_on(k, finish=False):
        own = k == 0 or k > items - CUTS
        j, h = order[k]
        for v, ref in enumerate((gk_ref, gv_ref)):
            src = ref.at[pl.ds((0 if k == 0 else k - items + CUTS) * cut, cut)] if own else grads.at[j, h, v]
            if not own and not finish:
                up(j, h, v, src).wait_recv()
            for copy, more in ((up, (j <= d) & (d < n - 1)), (down, (j >= d) & (d > 0))):
                @pl.when(more)
                def _(copy=copy, src=src, v=v):
                    if finish:
                        copy(j, h, v, src).wait_send()
                    else:
                        copy(j, h, v, src).start()

    def core_copy(k):
        return remote(c_send.at[k], c_recv.at[k], c_sem.at[0, k], c_sem.at[1, k], at_core)

    def x_copy(k):
        return remote(x_send.at[k], x_recv.at[k], x_sem.at[0, k], x_sem.at[1, k], at_x)

    def multiply(k):
        j, h = order[k]
        for sub in range(2):
            start = pl.multiple_of((1 - core) * half + sub * quarter, quarter)
            c_send[k, sub] = (
                nt_dot(grads[j, h, 0], weights[0, pl.ds(start, quarter), :])
                + nt_dot(grads[j, h, 1], weights[1, pl.ds(start, quarter), :])
            ).astype(BF16)
        core_copy(k).start()
        for sub in range(2):
            start = pl.multiple_of(core * half + sub * quarter, quarter)
            acc[k, sub] = (
                nt_dot(grads[j, h, 0], weights[0, pl.ds(start, quarter), :])
                + nt_dot(grads[j, h, 1], weights[1, pl.ds(start, quarter), :])
            )

    def add_core(k):
        core_copy(k).wait_recv()
        x_send[k] = (acc[k, 1 - x] + c_recv[k, 1 - x].astype(F32)).astype(BF16)
        x_copy(k).start()
        acc[k, x] = acc[k, x] + c_recv[k, x].astype(F32)

    def f_copy(k):
        i, h = order[k]
        return remote(f_send.at[k], f_recv.at[d, h], f_send_sem.at[k], f_recv_sem.at[d, h], (group, i, t))

    def add_x(k):
        x_copy(k).wait_recv()
        total = (acc[k, x] + x_recv[k].astype(F32)).astype(BF16)
        if k == 0 or k > items - CUTS:
            f_recv[d, 0 if k == 0 else k - items + CUTS] = total
        else:
            f_send[k] = total
            f_copy(k).start()

    columns = pl.ds(pl.multiple_of(core * half + x * quarter, quarter), quarter)

    def deliver(source, h, own=False, finish=False):
        if not own and not finish:
            remote(
                f_send.at[0], f_recv.at[source, h], f_send_sem.at[0], f_recv_sem.at[source, h], (group, source, t)
            ).wait_recv()
        there = out_ref.at[pl.ds(pl.multiple_of(h * cut, cut), cut), columns]

        @pl.when(source == t)
        def _():
            if not finish:
                pltpu.make_async_copy(f_recv.at[source, h], there, o_recv_sem.at[t, h]).start()

        @pl.when(source != t)
        def _():
            copy = remote(
                f_recv.at[source, h], there, o_send_sem.at[source, h], o_recv_sem.at[t, h], (group, d, source)
            )
            if finish:
                copy.wait_send()
            else:
                copy.start()

    def sk_copy(i, where):
        return remote(sk_send.at[i], sk_recv.at[i], sk_sem.at[0, i], sk_sem.at[1, i], where)

    def sketch_parts():
        for load in loads[6:9]:
            load.wait()
        sk_acc[:, : 2 * rank] = jnp.dot(normed[...], pin[...], preferred_element_type=F32)
        for h in range(CUTS):
            sk_acc[pl.ds(h * cut, cut), 2 * rank :] = jnp.concatenate(
                [nt_dot(grads[d, h, 0], pout[0]), nt_dot(grads[d, h, 1], pout[1])], axis=1
            )
        sk_send[0] = sk_acc[...].astype(BF16)
        sk_copy(0, at_core).start()

    def sketch_x():
        sk_copy(0, at_core).wait_recv()
        sk_acc[...] = sk_acc[...] + sk_recv[0].astype(F32)
        sk_send[1] = sk_acc[...].astype(BF16)
        sk_half(1, sk_send, core, at_x).start()

    def sk_half(i, src, part, where):
        span = pl.ds(pl.multiple_of(part * (rows // 2), rows // 2), rows // 2)
        return remote(src.at[1, span], sk_recv.at[1, span], sk_sem.at[0, i], sk_sem.at[1, i], where)

    def sketch_turn():
        sk_half(1, sk_send, core, at_x).wait_recv()
        sk_half(2, sk_recv, core, at_core).start()

    def seq_copy(step, source=None):
        slot = d if source is None else source
        return remote(
            seqs.at[slot], seqs.at[slot], s_send_sem.at[step], s_recv_sem.at[slot],
            (group, lax.rem(d + step, n), t),
        )

    def sketch_seq():
        sk_half(2, sk_recv, 1 - core, at_core).wait_recv()
        whole = (sk_acc[...] + sk_recv[1].astype(F32)).astype(BF16)
        length = length_ref[0]
        live = lax.broadcasted_iota(jnp.int32, (rows, 2 * rank), 0) < length
        outs = jnp.where(live, whole[:, 2 * rank :].astype(F32), 0.0).astype(BF16)
        c = lax.broadcasted_iota(jnp.int32, (2 * rank, 2 * own_rows), 0)
        r = lax.broadcasted_iota(jnp.int32, (2 * rank, 2 * own_rows), 1)
        chosen = (r // own_rows) * rank + t * own_rows + lax.rem(r, own_rows)
        mine = jnp.dot(outs, (c == chosen).astype(F32).astype(BF16), preferred_element_type=F32).astype(BF16)
        sums = lax.dot_general(
            mine, whole[:, : 2 * rank], (((0,), (0,)), ((), ())), preferred_element_type=F32
        )
        scale = 1.0 / jnp.sqrt(jnp.full(sums.shape, length, jnp.int32).astype(F32))
        seqs[d] = (sums * scale).astype(BF16)
        for step in range(1, n):
            seq_copy(step).start()

    def part_copy(step, source=None):
        slot = t if source is None else source
        return remote(
            parts.at[slot], parts.at[slot], p_send_sem.at[step], p_recv_sem.at[slot],
            (group, d, lax.rem(t + step, n)),
        )

    def part_scores():
        for step in range(1, n):
            seq_copy(step, lax.rem(d + step, n)).wait_recv()
        loads[9].wait()
        wide = 2 * own_rows * rank
        block = 2 * own_rows
        f = lax.broadcasted_iota(jnp.int32, (2 * rank, wide), 1)
        c = lax.broadcasted_iota(jnp.int32, (2 * rank, wide), 0)
        spread = (c == (f // (own_rows * rank)) * rank + lax.rem(f, rank)).astype(F32).astype(BF16)
        everything = jnp.concatenate([seqs[i] for i in range(n)], axis=0)
        tall = jnp.dot(everything, spread, preferred_element_type=F32)
        f = lax.broadcasted_iota(jnp.int32, (n * block, wide), 1)
        r = lax.broadcasted_iota(jnp.int32, (n * block, wide), 0)
        kept = jnp.where(lax.rem(r, block) == f // rank, tall, 0.0).astype(BF16)
        s = lax.broadcasted_iota(jnp.int32, (8, n * block), 0)
        r = lax.broadcasted_iota(jnp.int32, (8, n * block), 1)
        flat = jnp.dot((r // block == s).astype(F32).astype(BF16), kept, preferred_element_type=F32).astype(BF16)
        parts[t] = nt_dot(flat[:, : wide // 2], queries[:, 0, :]) + nt_dot(flat[:, wide // 2 :], queries[:, 1, :])
        for step in range(1, n):
            part_copy(step).start()

    def whole_scores():
        for step in range(1, n):
            part_copy(step, lax.rem(t + step, n)).wait_recv()
        total = parts[0]
        for i in range(1, n):
            total = total + parts[i]
        score_ref[...] = (total * (1.0 / rank))[:n]

    pass_on(0)
    for h in range(1, CUTS):
        pass_on(items - CUTS + h)
    for load in loads[:6]:
        load.wait()
    multiply(0)
    pass_on(1)
    add_core(0)
    multiply(items - 1)
    multiply(1)
    pass_on(2)
    sketch_parts()
    add_core(1)
    multiply(2)
    pass_on(3)
    sketch_x()
    add_core(2)
    multiply(3)
    add_x(0)
    add_x(1)
    pass_on(4)
    add_core(3)
    multiply(4)
    sketch_turn()
    add_x(2)
    pass_on(5)
    add_core(4)
    multiply(5)
    sketch_seq()
    add_x(3)
    pass_on(6)
    add_core(5)
    multiply(6)
    add_x(4)
    add_core(6)
    add_core(7)
    deliver(d, 0, own=True)
    deliver(*expected[0])
    add_x(5)
    deliver(*expected[1])
    add_x(6)
    add_x(7)
    deliver(d, 1, own=True)
    part_scores()
    deliver(*expected[2])
    deliver(*expected[3])
    deliver(*expected[4])
    deliver(*expected[5])
    whole_scores()
    for source in range(n):
        for h in range(CUTS):
            place = pl.ds(((source % 2) * 2 + source // 2) * quarter, quarter)
            remote(f_recv.at[0, h], out_ref.at[pl.ds(h * cut, cut), place],
                   o_send_sem.at[0, 0], o_recv_sem.at[source, h], at_core).wait_recv()
    for k in range(items):
        pass_on(k, finish=True)
        core_copy(k).wait_send()
        x_copy(k).wait_send()
        if 0 < k <= items - CUTS:
            f_copy(k).wait_send()
    for k in range(1, n):
        seq_copy(k).wait_send()
        part_copy(k).wait_send()
    for source in range(n):
        for h in range(CUTS):
            deliver(source, h, finish=True)
    sk_copy(0, at_core).wait_send()
    sk_half(1, sk_send, core, at_x).wait_send()
    sk_half(2, sk_recv, core, at_core).wait_send()


def body(
    normed, grad_key, grad_value, weight_key, weight_value, proj_in, proj_out, lengths, queries
):
    n = lax.axis_size("dp")
    rows, wide = normed.shape
    depth = grad_key.shape[1]
    rank = proj_out.shape[2]
    count = queries.shape[0]
    features = weight_key.shape[0]
    if not (n == lax.axis_size("tensor") == 4 and lengths.shape[0] == 1 and features == wide):
        return plain(
            normed, grad_key, grad_value, weight_key, weight_value, proj_in, proj_out, lengths, queries
        )
    quarter = features // 4
    items, cut = n * CUTS, rows // CUTS
    flat_queries = queries
    anywhere = pl.BlockSpec(memory_space=pl.ANY)
    dma = pltpu.SemaphoreType.DMA
    grad_input, scores = pl.pallas_call(
        lambda *refs: fused_kernel(n, *refs),
        out_shape=(
            jax.ShapeDtypeStruct((rows, wide), BF16),
            jax.ShapeDtypeStruct((n, count), F32),
        ),
        in_specs=[pl.BlockSpec(memory_space=pltpu.SMEM)] + [anywhere] * 8,
        out_specs=(anywhere, pl.BlockSpec(memory_space=pltpu.VMEM)),
        scratch_shapes=[
            pltpu.VMEM((n, CUTS, 2, cut, depth), BF16),
            pltpu.VMEM((2, features, depth), BF16),
            pltpu.VMEM(normed.shape, BF16),
            pltpu.VMEM(proj_in.shape, BF16),
            pltpu.VMEM((2, rank, depth), BF16),
            pltpu.VMEM(flat_queries.shape, BF16),
            pltpu.VMEM((items, 2, cut, quarter), F32),
            pltpu.VMEM((items, 2, cut, quarter), BF16),
            pltpu.VMEM((items, 2, cut, quarter), BF16),
            pltpu.VMEM((items, cut, quarter), BF16),
            pltpu.VMEM((items, cut, quarter), BF16),
            pltpu.VMEM((items, cut, quarter), BF16),
            pltpu.VMEM((n, CUTS, cut, quarter), BF16),
            pltpu.VMEM((rows, 4 * rank), F32),
            pltpu.VMEM((2, rows, 4 * rank), BF16),
            pltpu.VMEM((2, rows, 4 * rank), BF16),
            pltpu.VMEM((n, 2 * rank // n, 2 * rank), BF16),
            pltpu.VMEM((n, 8, count), F32),
            dma((10,)),
            dma((2, n, CUTS, 2)),
            dma((n, CUTS, 2)),
            dma((2, items)),
            dma((2, items)),
            dma((items,)),
            dma((n, CUTS)),
            dma((n, CUTS)),
            dma((n, CUTS)),
            dma((2, 3)),
            dma((n,)),
            dma((n,)),
            dma((n,)),
            dma((n,)),
        ],
        compiler_params=pltpu.CompilerParams(
            collective_id=0, has_side_effects=True, vmem_limit_bytes=62 * 1024 * 1024
        ),
    )(
        lengths, normed, grad_key, grad_value, weight_key, weight_value, proj_in,
        jnp.swapaxes(proj_out, 1, 2), flat_queries,
    )
    return (grad_input, scores.T)


def solution(mesh):
    in_specs = (
        P(("groups", "dp"), "tensor"),
        P(("groups", "dp"), "tensor"),
        P(("groups", "dp"), "tensor"),
        P("dp", "tensor"),
        P("dp", "tensor"),
        P("tensor", None),
        P(None, "tensor", None),
        P(("groups", "dp")),
        P("dp", None, "tensor"),
    )
    out_specs = (P(("groups", "dp"), "tensor"), P("dp", "groups"))
    return jax.shard_map(body, mesh=mesh, in_specs=in_specs, out_specs=out_specs, check_vma=False)
```

```python
import jax
import jax.numpy as jnp
from jax import lax
from jax.experimental import pallas as pl
from jax.experimental.pallas import tpu as pltpu
from jax.sharding import PartitionSpec as P


def by_tokens(grads, weights):
    partial_grad = lax.dot_general(
        grads,
        lax.all_gather(weights, "dp", axis=0, tiled=True),
        (((1,), (1,)), ((), ())),
        preferred_element_type=jnp.float32,
    )
    return lax.psum_scatter(
        partial_grad.astype(jnp.bfloat16), "tensor", scatter_dimension=1, tiled=True
    )


def by_features(grads, weights):
    n = lax.axis_size("dp")
    partial_grad = lax.dot_general(
        lax.all_gather(grads, "dp", axis=0, tiled=True),
        weights,
        (((1,), (1,)), ((), ())),
        preferred_element_type=jnp.float32,
    )
    mine = lax.psum_scatter(
        partial_grad.astype(jnp.bfloat16), "tensor", scatter_dimension=0, tiled=True
    )
    turn = [(d * n + t, t * n + d) for d in range(n) for t in range(n)]
    return lax.ppermute(mine, ("dp", "tensor"), turn)


def plain(
    normed, grad_key, grad_value, weight_key, weight_value, proj_in, proj_out, lengths, queries
):
    grads = jnp.concatenate([grad_key, grad_value], axis=1)
    weights = jnp.concatenate([weight_key, weight_value], axis=1)
    if lax.axis_size("dp") == lax.axis_size("tensor"):
        grad_input = by_features(grads, weights)
    else:
        grad_input = by_tokens(grads, weights)
    tokens = normed.shape[0]
    rank = proj_out.shape[2]
    shards = lax.axis_size("tensor")
    own_rows = rank // shards
    in_part = jnp.dot(normed, proj_in, preferred_element_type=jnp.float32)
    out_part = jnp.stack(
        [
            jnp.dot(grad_key, proj_out[0], preferred_element_type=jnp.float32),
            jnp.dot(grad_value, proj_out[1], preferred_element_type=jnp.float32),
        ],
        axis=1,
    )
    in_whole, out_whole = (
        lax.psum(in_part.astype(jnp.bfloat16), "tensor").astype(jnp.float32),
        lax.psum(out_part.astype(jnp.bfloat16), "tensor").astype(jnp.float32),
    )
    out_own = lax.dynamic_slice_in_dim(out_whole, lax.axis_index("tensor") * own_rows, own_rows, 2)
    in_sketch = in_whole.astype(jnp.bfloat16)
    out_sketch = out_own.astype(jnp.bfloat16)
    seq_count = lengths.shape[0]
    seq_len = tokens // seq_count
    positions = lax.broadcasted_iota(jnp.int32, (seq_count, seq_len), 1)
    live = (positions < lengths[:, None]).astype(jnp.bfloat16)
    in_seq = in_sketch.reshape(seq_count, seq_len, 2, rank)
    out_seq = out_sketch.reshape(seq_count, seq_len, 2, own_rows) * live[:, :, None, None]
    sums = jnp.einsum("stla,stlb->slab", out_seq, in_seq, preferred_element_type=jnp.float32)
    scale = 1.0 / jnp.sqrt(lengths.astype(jnp.float32))
    seq_sketch = (
        (sums * scale[:, None, None, None])
        .astype(jnp.bfloat16)
        .reshape(seq_count, 2, own_rows * rank)
    )
    partial_scores = jnp.einsum(
        "qlf,slf->qs",
        queries,
        lax.all_gather(seq_sketch, "dp", axis=0, tiled=True),
        preferred_element_type=jnp.float32,
    )
    scores = lax.psum(partial_scores, "tensor") / rank
    return (grad_input, scores)


MESH = pl.DeviceIdType.MESH
F32 = jnp.float32
BF16 = jnp.bfloat16


CUTS = 2


def visit(n):
    rows = []
    for d in range(n):
        far = [(j, h) for h in range(CUTS) for j in range(n) if j != d]
        far.sort(key=lambda item: ((abs(item[0] - d) - 1) * CUTS + item[1], min(item[0], n - 1 - item[0])))
        rows.append([(d, 0)] + far + [(d, h) for h in range(1, CUTS)])
    return rows


def arrivals(n):
    table = visit(n)
    rows = []
    for i in range(n):
        far = [(s, h) for s in range(n) if s != i for h in range(CUTS)]
        far.sort(key=lambda item: (table[item[0]].index((i, item[1])), abs(item[0] - i)))
        rows.append(far)
    return rows


def pick(table, d, k):
    values = []
    for part in range(2):
        value = jnp.int32(table[0][k][part])
        for place in range(1, len(table)):
            value = jnp.where(d == place, table[place][k][part], value)
        values.append(value)
    return values


def nt_dot(a, b):
    return lax.dot_general(a, b, (((1,), (1,)), ((), ())), preferred_element_type=F32)


def fused_kernel(
    n,
    length_ref, normed_ref, gk_ref, gv_ref, wk_ref, wv_ref, pin_ref, pout_ref, q_ref,
    out_ref, score_ref,
    grads, weights, normed, pin, pout, queries,
    acc, c_send, c_recv, x_send, x_recv, f_send, f_recv,
    sk_acc, sk_send, sk_recv, seqs, parts,
    load_sem, g_send_sem, g_recv_sem, c_sem, x_sem, f_send_sem, f_recv_sem,
    o_send_sem, o_recv_sem, sk_sem, s_send_sem, s_recv_sem, p_send_sem, p_recv_sem,
):
    group, d, t = lax.axis_index("groups"), lax.axis_index("dp"), lax.axis_index("tensor")
    core, x = lax.rem(t, 2), lax.div(t, 2)
    rows = gk_ref.shape[0]
    rank = pout_ref.shape[1]
    own_rows = rank // n
    half = wk_ref.shape[0] // 2
    quarter = half // 2
    table = visit(n)
    items = n * CUTS
    order = [pick(table, d, k) for k in range(items)]
    coming = arrivals(n)
    expected = [pick(coming, d, k) for k in range(items - CUTS)]
    cut = rows // CUTS
    at_core = (group, d, t + 1 - 2 * core)
    at_x = (group, d, lax.rem(t + 2, 4))

    def remote(src, dst, send, recv, where):
        return pltpu.make_async_remote_copy(
            src_ref=src, dst_ref=dst, send_sem=send, recv_sem=recv,
            device_id=where, device_id_type=MESH,
        )

    loads = [
        pltpu.make_async_copy(src, dst, load_sem.at[i])
        for i, (src, dst) in enumerate(
            [(src.at[pl.ds(h * cut, cut)], grads.at[d, h, v]) for v, src in enumerate((gk_ref, gv_ref)) for h in range(CUTS)]
            + [
                (wk_ref, weights.at[0]), (wv_ref, weights.at[1]),
                (normed_ref, normed), (pin_ref, pin), (pout_ref, pout), (q_ref, queries),
            ]
        )
    ]
    for load in loads:
        load.start()

    barrier = pltpu.get_barrier_semaphore()
    for step in range(1, n):
        pl.semaphore_signal(barrier, 1, device_id=(group, lax.rem(d + step, n), t), device_id_type=MESH)
        pl.semaphore_signal(barrier, 1, device_id=(group, d, lax.rem(t + step, n)), device_id_type=MESH)
    pl.semaphore_wait(barrier, 2 * (n - 1))

    def up(j, h, v, src):
        return remote(
            src, grads.at[j, h, v], g_send_sem.at[0, j, h, v], g_recv_sem.at[j, h, v], (group, lax.rem(d + 1, n), t)
        )

    def down(j, h, v, src):
        return remote(
            src, grads.at[j, h, v], g_send_sem.at[1, j, h, v], g_recv_sem.at[j, h, v], (group, lax.rem(d + n - 1, n), t)
        )

    def pass_on(k, finish=False):
        own = k == 0 or k > items - CUTS
        j, h = order[k]
        for v, ref in enumerate((gk_ref, gv_ref)):
            src = ref.at[pl.ds((0 if k == 0 else k - items + CUTS) * cut, cut)] if own else grads.at[j, h, v]
            if not own and not finish:
                up(j, h, v, src).wait_recv()
            for copy, more in ((up, (j <= d) & (d < n - 1)), (down, (j >= d) & (d > 0))):
                @pl.when(more)
                def _(copy=copy, src=src, v=v):
                    if finish:
                        copy(j, h, v, src).wait_send()
                    else:
                        copy(j, h, v, src).start()

    def core_copy(k):
        return remote(c_send.at[k], c_recv.at[k], c_sem.at[0, k], c_sem.at[1, k], at_core)

    def x_copy(k):
        return remote(x_send.at[k], x_recv.at[k], x_sem.at[0, k], x_sem.at[1, k], at_x)

    def multiply(k):
        j, h = order[k]
        for sub in range(2):
            start = pl.multiple_of((1 - core) * half + sub * quarter, quarter)
            c_send[k, sub] = (
                nt_dot(grads[j, h, 0], weights[0, pl.ds(start, quarter), :])
                + nt_dot(grads[j, h, 1], weights[1, pl.ds(start, quarter), :])
            ).astype(BF16)
        core_copy(k).start()
        for sub in range(2):
            start = pl.multiple_of(core * half + sub * quarter, quarter)
            acc[k, sub] = (
                nt_dot(grads[j, h, 0], weights[0, pl.ds(start, quarter), :])
                + nt_dot(grads[j, h, 1], weights[1, pl.ds(start, quarter), :])
            )

    def add_core(k):
        core_copy(k).wait_recv()
        x_send[k] = (acc[k, 1 - x] + c_recv[k, 1 - x].astype(F32)).astype(BF16)
        x_copy(k).start()
        acc[k, x] = acc[k, x] + c_recv[k, x].astype(F32)

    def f_copy(k):
        i, h = order[k]
        return remote(f_send.at[k], f_recv.at[d, h], f_send_sem.at[k], f_recv_sem.at[d, h], (group, i, t))

    def add_x(k):
        x_copy(k).wait_recv()
        total = (acc[k, x] + x_recv[k].astype(F32)).astype(BF16)
        if k == 0 or k > items - CUTS:
            f_recv[d, 0 if k == 0 else k - items + CUTS] = total
        else:
            f_send[k] = total
            f_copy(k).start()

    columns = pl.ds(pl.multiple_of(core * half + x * quarter, quarter), quarter)

    def deliver(source, h, own=False, finish=False):
        if not own and not finish:
            remote(
                f_send.at[0], f_recv.at[source, h], f_send_sem.at[0], f_recv_sem.at[source, h], (group, source, t)
            ).wait_recv()
        there = out_ref.at[pl.ds(pl.multiple_of(h * cut, cut), cut), columns]

        @pl.when(source == t)
        def _():
            if not finish:
                pltpu.make_async_copy(f_recv.at[source, h], there, o_recv_sem.at[t, h]).start()

        @pl.when(source != t)
        def _():
            copy = remote(
                f_recv.at[source, h], there, o_send_sem.at[source, h], o_recv_sem.at[t, h], (group, d, source)
            )
            if finish:
                copy.wait_send()
            else:
                copy.start()

    def sk_copy(i, where):
        return remote(sk_send.at[i], sk_recv.at[i], sk_sem.at[0, i], sk_sem.at[1, i], where)

    def sketch_parts():
        for load in loads[6:9]:
            load.wait()
        sk_acc[:, : 2 * rank] = jnp.dot(normed[...], pin[...], preferred_element_type=F32)
        for h in range(CUTS):
            sk_acc[pl.ds(h * cut, cut), 2 * rank :] = jnp.concatenate(
                [nt_dot(grads[d, h, 0], pout[0]), nt_dot(grads[d, h, 1], pout[1])], axis=1
            )
        sk_send[0] = sk_acc[...].astype(BF16)
        sk_copy(0, at_core).start()

    def sketch_x():
        sk_copy(0, at_core).wait_recv()
        sk_acc[...] = sk_acc[...] + sk_recv[0].astype(F32)
        sk_send[1] = sk_acc[...].astype(BF16)
        sk_half(1, sk_send, core, at_x).start()

    def sk_half(i, src, part, where):
        span = pl.ds(pl.multiple_of(part * (rows // 2), rows // 2), rows // 2)
        return remote(src.at[1, span], sk_recv.at[1, span], sk_sem.at[0, i], sk_sem.at[1, i], where)

    def sketch_turn():
        sk_half(1, sk_send, core, at_x).wait_recv()
        sk_half(2, sk_recv, core, at_core).start()

    def seq_copy(step, source=None):
        slot = d if source is None else source
        return remote(
            seqs.at[slot], seqs.at[slot], s_send_sem.at[step], s_recv_sem.at[slot],
            (group, lax.rem(d + step, n), t),
        )

    def sketch_seq():
        sk_half(2, sk_recv, 1 - core, at_core).wait_recv()
        whole = (sk_acc[...] + sk_recv[1].astype(F32)).astype(BF16)
        length = length_ref[0]
        live = lax.broadcasted_iota(jnp.int32, (rows, 2 * rank), 0) < length
        outs = jnp.where(live, whole[:, 2 * rank :].astype(F32), 0.0).astype(BF16)
        c = lax.broadcasted_iota(jnp.int32, (2 * rank, 2 * own_rows), 0)
        r = lax.broadcasted_iota(jnp.int32, (2 * rank, 2 * own_rows), 1)
        chosen = (r // own_rows) * rank + t * own_rows + lax.rem(r, own_rows)
        mine = jnp.dot(outs, (c == chosen).astype(F32).astype(BF16), preferred_element_type=F32).astype(BF16)
        sums = lax.dot_general(
            mine, whole[:, : 2 * rank], (((0,), (0,)), ((), ())), preferred_element_type=F32
        )
        scale = 1.0 / jnp.sqrt(jnp.full(sums.shape, length, jnp.int32).astype(F32))
        seqs[d] = (sums * scale).astype(BF16)
        for step in range(1, n):
            seq_copy(step).start()

    def part_copy(step, source=None):
        slot = t if source is None else source
        return remote(
            parts.at[slot], parts.at[slot], p_send_sem.at[step], p_recv_sem.at[slot],
            (group, d, lax.rem(t + step, n)),
        )

    def part_scores():
        for step in range(1, n):
            seq_copy(step, lax.rem(d + step, n)).wait_recv()
        loads[9].wait()
        wide = 2 * own_rows * rank
        block = 2 * own_rows
        f = lax.broadcasted_iota(jnp.int32, (2 * rank, wide), 1)
        c = lax.broadcasted_iota(jnp.int32, (2 * rank, wide), 0)
        spread = (c == (f // (own_rows * rank)) * rank + lax.rem(f, rank)).astype(F32).astype(BF16)
        everything = jnp.concatenate([seqs[i] for i in range(n)], axis=0)
        tall = jnp.dot(everything, spread, preferred_element_type=F32)
        f = lax.broadcasted_iota(jnp.int32, (n * block, wide), 1)
        r = lax.broadcasted_iota(jnp.int32, (n * block, wide), 0)
        kept = jnp.where(lax.rem(r, block) == f // rank, tall, 0.0).astype(BF16)
        s = lax.broadcasted_iota(jnp.int32, (8, n * block), 0)
        r = lax.broadcasted_iota(jnp.int32, (8, n * block), 1)
        flat = jnp.dot((r // block == s).astype(F32).astype(BF16), kept, preferred_element_type=F32).astype(BF16)
        parts[t] = nt_dot(flat[:, : wide // 2], queries[:, 0, :]) + nt_dot(flat[:, wide // 2 :], queries[:, 1, :])
        for step in range(1, n):
            part_copy(step).start()

    def whole_scores():
        for step in range(1, n):
            part_copy(step, lax.rem(t + step, n)).wait_recv()
        total = parts[0]
        for i in range(1, n):
            total = total + parts[i]
        score_ref[...] = (total * (1.0 / rank))[:n]

    pass_on(0)
    for h in range(1, CUTS):
        pass_on(items - CUTS + h)
    for load in loads[:6]:
        load.wait()
    multiply(0)
    pass_on(1)
    add_core(0)
    multiply(items - 1)
    multiply(1)
    pass_on(2)
    sketch_parts()
    add_core(1)
    multiply(2)
    pass_on(3)
    sketch_x()
    add_core(2)
    multiply(3)
    add_x(0)
    add_x(1)
    pass_on(4)
    add_core(3)
    multiply(4)
    sketch_turn()
    add_x(2)
    pass_on(5)
    add_core(4)
    multiply(5)
    sketch_seq()
    add_x(3)
    pass_on(6)
    add_core(5)
    multiply(6)
    add_x(4)
    add_core(6)
    add_core(7)
    add_x(5)
    add_x(6)
    deliver(*expected[0])
    deliver(*expected[1])
    deliver(d, 0, own=True)
    add_x(7)
    deliver(*expected[2])
    deliver(*expected[3])
    part_scores()
    deliver(*expected[4])
    deliver(*expected[5])
    deliver(d, 1, own=True)
    whole_scores()
    for source in range(n):
        for h in range(CUTS):
            place = pl.ds(((source % 2) * 2 + source // 2) * quarter, quarter)
            remote(f_recv.at[0, h], out_ref.at[pl.ds(h * cut, cut), place],
                   o_send_sem.at[0, 0], o_recv_sem.at[source, h], at_core).wait_recv()
    for k in range(items):
        pass_on(k, finish=True)
        core_copy(k).wait_send()
        x_copy(k).wait_send()
        if 0 < k <= items - CUTS:
            f_copy(k).wait_send()
    for k in range(1, n):
        seq_copy(k).wait_send()
        part_copy(k).wait_send()
    for source in range(n):
        for h in range(CUTS):
            deliver(source, h, finish=True)
    sk_copy(0, at_core).wait_send()
    sk_half(1, sk_send, core, at_x).wait_send()
    sk_half(2, sk_recv, core, at_core).wait_send()


def body(
    normed, grad_key, grad_value, weight_key, weight_value, proj_in, proj_out, lengths, queries
):
    n = lax.axis_size("dp")
    rows, wide = normed.shape
    depth = grad_key.shape[1]
    rank = proj_out.shape[2]
    count = queries.shape[0]
    features = weight_key.shape[0]
    if not (n == lax.axis_size("tensor") == 4 and lengths.shape[0] == 1 and features == wide):
        return plain(
            normed, grad_key, grad_value, weight_key, weight_value, proj_in, proj_out, lengths, queries
        )
    quarter = features // 4
    items, cut = n * CUTS, rows // CUTS
    flat_queries = queries
    anywhere = pl.BlockSpec(memory_space=pl.ANY)
    dma = pltpu.SemaphoreType.DMA
    grad_input, scores = pl.pallas_call(
        lambda *refs: fused_kernel(n, *refs),
        out_shape=(
            jax.ShapeDtypeStruct((rows, wide), BF16),
            jax.ShapeDtypeStruct((n, count), F32),
        ),
        in_specs=[pl.BlockSpec(memory_space=pltpu.SMEM)] + [anywhere] * 8,
        out_specs=(anywhere, pl.BlockSpec(memory_space=pltpu.VMEM)),
        scratch_shapes=[
            pltpu.VMEM((n, CUTS, 2, cut, depth), BF16),
            pltpu.VMEM((2, features, depth), BF16),
            pltpu.VMEM(normed.shape, BF16),
            pltpu.VMEM(proj_in.shape, BF16),
            pltpu.VMEM((2, rank, depth), BF16),
            pltpu.VMEM(flat_queries.shape, BF16),
            pltpu.VMEM((items, 2, cut, quarter), F32),
            pltpu.VMEM((items, 2, cut, quarter), BF16),
            pltpu.VMEM((items, 2, cut, quarter), BF16),
            pltpu.VMEM((items, cut, quarter), BF16),
            pltpu.VMEM((items, cut, quarter), BF16),
            pltpu.VMEM((items, cut, quarter), BF16),
            pltpu.VMEM((n, CUTS, cut, quarter), BF16),
            pltpu.VMEM((rows, 4 * rank), F32),
            pltpu.VMEM((2, rows, 4 * rank), BF16),
            pltpu.VMEM((2, rows, 4 * rank), BF16),
            pltpu.VMEM((n, 2 * rank // n, 2 * rank), BF16),
            pltpu.VMEM((n, 8, count), F32),
            dma((10,)),
            dma((2, n, CUTS, 2)),
            dma((n, CUTS, 2)),
            dma((2, items)),
            dma((2, items)),
            dma((items,)),
            dma((n, CUTS)),
            dma((n, CUTS)),
            dma((n, CUTS)),
            dma((2, 3)),
            dma((n,)),
            dma((n,)),
            dma((n,)),
            dma((n,)),
        ],
        compiler_params=pltpu.CompilerParams(
            collective_id=0, has_side_effects=True, vmem_limit_bytes=62 * 1024 * 1024
        ),
    )(
        lengths, normed, grad_key, grad_value, weight_key, weight_value, proj_in,
        jnp.swapaxes(proj_out, 1, 2), flat_queries,
    )
    return (grad_input, scores.T)


def solution(mesh):
    in_specs = (
        P(("groups", "dp"), "tensor"),
        P(("groups", "dp"), "tensor"),
        P(("groups", "dp"), "tensor"),
        P("dp", "tensor"),
        P("dp", "tensor"),
        P("tensor", None),
        P(None, "tensor", None),
        P(("groups", "dp")),
        P("dp", None, "tensor"),
    )
    out_specs = (P(("groups", "dp"), "tensor"), P("dp", "groups"))
    return jax.shard_map(body, mesh=mesh, in_specs=in_specs, out_specs=out_specs, check_vma=False)
```
